256 devices in a mesh: dp: 16 (over y, z_hi), tensor: 16 (over x, z_lo, core).
Axes of the slice: x: 4, y: 4, z: 8 (z_hi: 4, z_lo: 2; z = z_hi * 2 + z_lo), core: 2. Of those that a mesh axis runs over, the one named last changes fastest.
Arguments:
- attention_output: bfloat16 [8192, 8192], P('dp', 'tensor'), may hold values from -6 to 6
- frozen_weight: bfloat16 [8192, 8192], P('tensor'), may hold values from -0.0625 to 0.0625
- output_gradient: bfloat16 [8192, 8192], P('dp', 'tensor'), may hold values from -6 to 6
- tenant_token_count: int32 [16, 64], P('dp'), may hold values from 1 to 256, 512 in all within a row
- tenant_storage_slot: int32 [64], replicated, may hold values from 0 to 63, each once
- adapter_down_weight: float32 [64, 8192, 16], P('dp', 'tensor'), may hold values from -0.0625 to 0.0625
- adapter_up_weight: float32 [64, 16, 8192], P('dp', None, 'tensor'), may hold values from -1.5 to 1.5
- down_first_moment: float32 [64, 8192, 16], P('dp', 'tensor'), may hold values from -60 to 60
- down_second_moment: float32 [64, 8192, 16], P('dp', 'tensor'), may hold values from 1 to 10000
- up_first_moment: float32 [64, 16, 8192], P('dp', None, 'tensor'), may hold values from -60 to 60
- up_second_moment: float32 [64, 16, 8192], P('dp', None, 'tensor'), may hold values from 1 to 10000
Outputs:
- proj_out: bfloat16 [8192, 8192], P('dp', 'tensor')
- input_grad: bfloat16 [8192, 8192], P('dp', 'tensor')
- updated_down_weight: float32 [64, 8192, 16], P('dp', 'tensor')
- updated_up_weight: float32 [64, 16, 8192], P('dp', None, 'tensor')
- updated_down_first_moment: float32 [64, 8192, 16], P('dp', 'tensor')
- updated_down_second_moment: float32 [64, 8192, 16], P('dp', 'tensor')
- updated_up_first_moment: float32 [64, 16, 8192], P('dp', None, 'tensor')
- updated_up_second_moment: float32 [64, 16, 8192], P('dp', None, 'tensor')
The draws below stay inside these ranges and needn't reach their ends.
Inputs may be any that keep to these rules, and one draw needn't show every extreme that they name: `tenant_token_count`: each row sums to 512; every tenant has at least one token in every row; tokens of one dp index are sorted by tenant. `tenant_storage_slot`: a permutation of the slots.
All inputs are finite; a program needn't handle non-finite values.
Results may differ from the reference program's by a relative error of at most 0.02.
Values may be sent and summed in bfloat16 or wider, within the bound.
No kernel may reach another device: no remote copies, remote signals or barrier semaphores. Data moves between devices by JAX's collectives and lax.ppermute only.
A program may use at most 128 MiB of HBM per device.

```python
import math
import jax
import jax.numpy as jnp
import numpy as np
from jax import lax

MODEL_WIDTH = 8192
ADAPTER_RANK = 16
TOK_DEV = 512
TENANT_TOTAL = 64
TOKENS = 8192
N_DP = 16
N_TENSOR = 16


def block_scale(stream_key, dims, cuts, low, top_value):
    factor_of, own = 1.0, jax.random.fold_in(stream_key, 6)
    for position, parts in cuts:
        steps = jnp.exp(jax.random.uniform(jax.random.fold_in(own, position), (parts,), jnp.float32, low / len(cuts), top_value / len(cuts)))
        factor_of = factor_of * jnp.repeat(steps, dims[position] // parts).reshape([-1 if axis == position else 1 for axis in range(len(dims))])
    return factor_of


def length_profile(number_of, total, limit, slope):
    loads = [(1 << 20) // math.isqrt(standing ** slope) + 1 for standing in range(2, number_of + 1)]
    rest, counts = total - limit - (number_of - 1), [1] * (number_of - 1)
    while rest > 0:
        candidates = [i for i in range(number_of - 1) if counts[i] < limit]
        mass, budget = sum([loads[i] for i in candidates]), rest
        for i in candidates:
            more = min(limit - counts[i], max(1, budget * loads[i] // mass), rest)
            counts[i] = counts[i] + more
            rest = rest - more
    return np.array([limit] + counts)


def ragged(rng, number_of, total, bound, lean):
    if number_of == 2:
        one = jax.random.randint(rng, (), max(1, total - bound), min(bound, total - 1) + 1)
        return jnp.stack([one, total - one])
    tallies = jnp.asarray(length_profile(number_of, total, bound, lean), jnp.int32)
    pairs = (number_of - 1) // 2
    giver, taker = tallies[1:1 + 2 * pairs:2], tallies[2:2 + 2 * pairs:2]
    slack = jnp.minimum(giver - 1, bound - taker)
    passed = jax.random.randint(jax.random.fold_in(rng, 1), (pairs,), 0, 1 << 20) % (slack + 1)
    tallies = tallies.at[1:1 + 2 * pairs:2].set(giver - passed).at[2:2 + 2 * pairs:2].set(taker + passed)
    return tallies[jax.random.permutation(jax.random.fold_in(rng, 2), number_of)]


def bell_draw(own_key, shape, scale, most, split=(), kind=jnp.bfloat16):
    gain = block_scale(own_key, shape, split, -0.22, 0.18) if split else 1.0
    array = jax.random.normal(own_key, shape, jnp.float32) * scale * gain
    return jnp.minimum(jnp.maximum(array, -most), most).astype(kind)


def setup_inputs(seed: int = 0) -> dict:
    keys = jax.random.split(jax.random.key(seed), 12)
    attention_output = bell_draw(keys[0], (TOKENS, MODEL_WIDTH), 1.0, 6.0, ((0, 16), (1, 16)))
    frozen_weight = bell_draw(keys[1], (MODEL_WIDTH, MODEL_WIDTH), MODEL_WIDTH ** -0.5, 0.0625, ((0, 16),))
    output_gradient = bell_draw(keys[2], (TOKENS, MODEL_WIDTH), 1.0, 6.0, ((0, 16), (1, 16)))
    tenant_token_count = jax.vmap(lambda own: ragged(own, TENANT_TOTAL, TOK_DEV, TOK_DEV // 2, 2))(jax.random.split(keys[3], N_DP)).reshape((N_DP, TENANT_TOTAL)).astype(jnp.int32)
    tenant_storage_slot = jax.random.permutation(keys[4], TENANT_TOTAL).astype(jnp.int32)
    adapter_down_weight = bell_draw(keys[5], (TENANT_TOTAL, MODEL_WIDTH, ADAPTER_RANK), MODEL_WIDTH ** -0.5, 0.0625, ((0, 16), (1, 16)), jnp.float32)
    adapter_up_weight = bell_draw(keys[6], (TENANT_TOTAL, ADAPTER_RANK, MODEL_WIDTH), ADAPTER_RANK ** -0.5, 1.5, ((0, 16), (2, 16)), jnp.float32)
    down_first_moment = bell_draw(keys[7], (TENANT_TOTAL, MODEL_WIDTH, ADAPTER_RANK), 10.0, 60.0, ((0, 16), (1, 16)), jnp.float32)
    down_second_moment = jnp.clip(jnp.exp(math.log(10000.0) - 9.2103404 * jax.random.uniform(keys[8], (TENANT_TOTAL, MODEL_WIDTH, ADAPTER_RANK), jnp.float32) ** block_scale(keys[8], (TENANT_TOTAL, MODEL_WIDTH, ADAPTER_RANK), ((0, 16), (1, 16)), -0.2, 0.2)), 1.0, 10000.0)
    up_first_moment = bell_draw(keys[9], (TENANT_TOTAL, ADAPTER_RANK, MODEL_WIDTH), 10.0, 60.0, ((0, 16), (2, 16)), jnp.float32)
    up_second_moment = jnp.clip(jnp.exp(math.log(10000.0) - 9.2103404 * jax.random.uniform(keys[10], (TENANT_TOTAL, ADAPTER_RANK, MODEL_WIDTH), jnp.float32) ** block_scale(keys[10], (TENANT_TOTAL, ADAPTER_RANK, MODEL_WIDTH), ((0, 16), (2, 16)), -0.2, 0.2)), 1.0, 10000.0)
    return {"attention_output": attention_output, "frozen_weight": frozen_weight, "output_gradient": output_gradient, "tenant_token_count": tenant_token_count, "tenant_storage_slot": tenant_storage_slot, "adapter_down_weight": adapter_down_weight, "adapter_up_weight": adapter_up_weight, "down_first_moment": down_first_moment, "down_second_moment": down_second_moment, "up_first_moment": up_first_moment, "up_second_moment": up_second_moment}


def adam_update(param, first, second, grad):
    first = 0.9 * first + 0.1 * grad
    second = 0.999 * second + 0.001 * grad * grad
    corr_one = 1.0 - 0.9 ** 10
    corr_two = 1.0 - 0.999 ** 10
    step_size = first / corr_one / (jnp.sqrt(second / corr_two) + 1e-08)
    return (param - 0.01 * (step_size + 0.1 * param), first, second)

def reference(attention_output, frozen_weight, output_gradient, tenant_token_count, tenant_storage_slot, adapter_down_weight, adapter_up_weight, down_first_moment, down_second_moment, up_first_moment, up_second_moment):
    positions = jnp.arange(TOK_DEV, dtype=jnp.int32)
    ends = jnp.cumsum(tenant_token_count, axis=1)
    tenant = lax.optimization_barrier(jnp.sum((ends[:, None, :] <= positions[None, :, None]).astype(jnp.int32), axis=-1)).reshape(-1)
    slot = tenant_storage_slot[tenant]
    onehot = (slot[:, None] == jnp.arange(TENANT_TOTAL, dtype=jnp.int32)[None, :]).astype(jnp.float32)
    down_half_precision = adapter_down_weight.astype(jnp.bfloat16)
    up_half_precision = adapter_up_weight.astype(jnp.bfloat16)
    down_flat = jnp.transpose(down_half_precision, (1, 0, 2)).reshape(MODEL_WIDTH, TENANT_TOTAL * ADAPTER_RANK)
    up_flat = up_half_precision.reshape(TENANT_TOTAL * ADAPTER_RANK, MODEL_WIDTH)
    low_all = jnp.dot(attention_output, down_flat, preferred_element_type=jnp.float32).reshape(-1, TENANT_TOTAL, ADAPTER_RANK)
    low = lax.optimization_barrier(jnp.sum(low_all * onehot[:, :, None], axis=1))
    low_wide = (onehot[:, :, None] * low[:, None, :]).reshape(-1, TENANT_TOTAL * ADAPTER_RANK).astype(jnp.bfloat16)
    width = MODEL_WIDTH // N_TENSOR

    def add_block(total, index):
        cols = lax.dynamic_slice_in_dim(attention_output, index * width, width, 1)
        rows = lax.dynamic_slice_in_dim(frozen_weight, index * width, width, 0)
        part = lax.optimization_barrier(jnp.dot(cols, rows, preferred_element_type=jnp.float32).astype(jnp.bfloat16))
        return (total + part.astype(jnp.float32), None)
    base, _ = lax.scan(add_block, jnp.zeros((TOKENS, MODEL_WIDTH), jnp.float32), jnp.arange(N_TENSOR, dtype=jnp.int32))
    proj_out = (base + 2.0 * jnp.dot(low_wide, up_flat, preferred_element_type=jnp.float32)).astype(jnp.bfloat16)
    back_all = lax.dot_general(output_gradient, up_flat, (((1,), (1,)), ((), ())), preferred_element_type=jnp.float32).reshape(-1, TENANT_TOTAL, ADAPTER_RANK)
    back = lax.optimization_barrier(jnp.sum(back_all * onehot[:, :, None], axis=1))
    back_wide = (onehot[:, :, None] * back[:, None, :]).reshape(-1, TENANT_TOTAL * ADAPTER_RANK).astype(jnp.bfloat16)
    grad_base = lax.dot_general(output_gradient, frozen_weight, (((1,), (1,)), ((), ())), preferred_element_type=jnp.float32)
    grad_low = lax.dot_general(back_wide, down_flat, (((1,), (1,)), ((), ())), preferred_element_type=jnp.float32)
    input_grad = (grad_base + 2.0 * grad_low).astype(jnp.bfloat16)
    down_gradient = 2.0 * lax.dot_general(attention_output, back_wide, (((0,), (0,)), ((), ())), preferred_element_type=jnp.float32)
    down_gradient = jnp.transpose(down_gradient.reshape(MODEL_WIDTH, TENANT_TOTAL, ADAPTER_RANK), (1, 0, 2))
    up_gradient = 2.0 * lax.dot_general(low_wide, output_gradient, (((0,), (0,)), ((), ())), preferred_element_type=jnp.float32)
    up_gradient = up_gradient.reshape(TENANT_TOTAL, ADAPTER_RANK, MODEL_WIDTH)
    updated_down_weight, updated_down_first_moment, updated_down_second_moment = adam_update(adapter_down_weight, down_first_moment, down_second_moment, down_gradient)
    updated_up_weight, updated_up_first_moment, updated_up_second_moment = adam_update(adapter_up_weight, up_first_moment, up_second_moment, up_gradient)
    return (proj_out, input_grad, updated_down_weight, updated_up_weight, updated_down_first_moment, updated_down_second_moment, updated_up_first_moment, updated_up_second_moment)
```

```python
import functools

import jax
import jax.numpy as jnp
from jax import lax
from jax.experimental import pallas as pl
from jax.experimental.pallas import tpu as pltpu
from jax.sharding import Mesh
from jax.sharding import PartitionSpec as P

DP = ("y", "zh")
TENSOR = ("x", "zl", "c")
BF = jnp.bfloat16
F32 = jnp.float32
RING = (0, 3, 1, 2)
VMEM_LIMIT = 48 * 1024 * 1024


def send(a, axis, step):
    n = lax.axis_size(axis)
    return lax.ppermute(a, axis, [(i, (i + step) % n) for i in range(n)])


def nn(a, b):
    return lax.dot_general(a, b, (((1,), (0,)), ((), ())), preferred_element_type=F32)


def nt(a, b):
    return lax.dot_general(a, b, (((1,), (1,)), ((), ())), preferred_element_type=F32)


def tn(a, b):
    return lax.dot_general(a, b, (((0,), (0,)), ((), ())), preferred_element_type=F32)


def call(body, out, ins, flops=0):
    size = sum(a.size * a.dtype.itemsize for a in ins) + sum(o.size * o.dtype.itemsize for o in out)
    return pl.pallas_call(
        body,
        out_shape=out,
        in_specs=[pl.BlockSpec(memory_space=pltpu.VMEM)] * len(ins),
        out_specs=[pl.BlockSpec(memory_space=pltpu.VMEM)] * len(out),
        compiler_params=pltpu.CompilerParams(vmem_limit_bytes=VMEM_LIMIT),
        cost_estimate=pl.CostEstimate(flops=flops, bytes_accessed=size, transcendentals=0),
    )(*ins)


def shape(rows, cols, dtype):
    return jax.ShapeDtypeStruct((rows, cols), dtype)


def mask_body(rank, per, slots_ref, counts_ref, place_ref, out_ref):
    rows, toks = out_ref.shape
    tenants = slots_ref.shape[1]
    row = lax.broadcasted_iota(jnp.int32, (rows, 1), 0)
    block = row // (rank * per)
    y = block // 4
    z = block - 4 * y
    ring_y = jnp.where(y == 1, 3, jnp.where(y == 2, 1, jnp.where(y == 3, 2, 0)))
    ring_z = jnp.where(z == 1, 3, jnp.where(z == 2, 1, jnp.where(z == 3, 2, 0)))
    at = ((place_ref[0] + ring_y) % 4) * 4 + (place_ref[1] + ring_z) % 4
    slot = at * per + (row // rank) % per
    lane = lax.broadcasted_iota(jnp.int32, (rows, tenants), 1).astype(F32)
    counts = counts_ref[...].astype(F32)
    hit = jnp.where(slots_ref[...] == slot, 1.0, 0.0)
    tenant = jnp.sum(hit * lane, axis=1, keepdims=True)
    first = jnp.sum(jnp.where(lane < tenant, counts, 0.0), axis=1, keepdims=True)
    last = first + jnp.sum(hit * counts, axis=1, keepdims=True)
    tok = lax.broadcasted_iota(jnp.int32, (1, toks), 1).astype(F32)
    for r in range(0, rows, 256):
        inside = (tok >= first[r : r + 256]) & (tok < last[r : r + 256])
        out_ref[r : r + 256] = jnp.where(inside, 1.0, 0.0).astype(BF)


def token_mask(slots, counts, place, rank, per, toks):
    rows = slots.shape[0] * rank
    return pl.pallas_call(
        functools.partial(mask_body, rank, per),
        out_shape=shape(rows, toks, BF),
        in_specs=[
            pl.BlockSpec(memory_space=pltpu.VMEM),
            pl.BlockSpec(memory_space=pltpu.VMEM),
            pl.BlockSpec(memory_space=pltpu.SMEM),
        ],
        out_specs=pl.BlockSpec(memory_space=pltpu.VMEM),
        compiler_params=pltpu.CompilerParams(vmem_limit_bytes=VMEM_LIMIT),
        cost_estimate=pl.CostEstimate(flops=0, bytes_accessed=rows * toks * 4, transcendentals=0),
    )(slots.reshape(1, -1), counts, place)


def narrow_body(rank, x_ref, dy_ref, m_ref, own_ref, left_ref, right_ref, far_d_ref, far_u_ref, out_ref):
    n = far_d_ref.shape[0]
    x, dy = x_ref[...], dy_ref[...]
    downs = [own_ref[:n], left_ref[:n], right_ref[:n], far_d_ref[...]]
    ups = [own_ref[n:], left_ref[n:], right_ref[n:], far_u_ref[...]]
    for k, (side, blocks) in enumerate(((x, downs), (dy, ups))):
        total = None
        for g, block in enumerate(blocks):
            wide = nt(block, side) * m_ref[g * n : (g + 1) * n].astype(F32)
            part = jnp.sum(wide.reshape(n // rank, rank, wide.shape[1]), axis=0)
            total = part if total is None else total + part
        out_ref[k * rank : (k + 1) * rank] = total


def widen(lb_ref, m_ref, g, n, which, rank):
    narrow = lb_ref[which * rank : (which + 1) * rank].astype(BF)
    return jnp.concatenate([narrow] * (n // rank), axis=0) * m_ref[g * n : (g + 1) * n]


def grad_far_body(rank, x_ref, dy_ref, m_ref, lb_ref, down_ref, up_ref):
    n = down_ref.shape[0]
    down_ref[...] = (2.0 * nn(widen(lb_ref, m_ref, 3, n, 1, rank), x_ref[...])).astype(BF)
    up_ref[...] = (2.0 * nn(widen(lb_ref, m_ref, 3, n, 0, rank), dy_ref[...])).astype(BF)


def grad_near_body(rank, x_ref, dy_ref, m_ref, lb_ref, got_down_ref, got_up_ref, left_ref, right_ref):
    n = got_down_ref.shape[0]
    x, dy = x_ref[...], dy_ref[...]
    left_ref[:n] = (2.0 * nn(widen(lb_ref, m_ref, 1, n, 1, rank), x)).astype(BF)
    left_ref[n:] = (
        2.0 * nn(widen(lb_ref, m_ref, 1, n, 0, rank), dy) + got_up_ref[...].astype(F32)
    ).astype(BF)
    right_ref[:n] = (
        2.0 * nn(widen(lb_ref, m_ref, 2, n, 1, rank), x) + got_down_ref[...].astype(F32)
    ).astype(BF)
    right_ref[n:] = (2.0 * nn(widen(lb_ref, m_ref, 2, n, 0, rank), dy)).astype(BF)


def grad_own_body(
    rank, x_ref, dy_ref, m_ref, lb_ref, a_ref, b_ref, fd_ref, fu_ref, left_ref, right_ref, own_ref
):
    n = a_ref.shape[0] // 2
    q = n // 4
    for k, side in ((0, x_ref), (1, dy_ref)):
        rows = slice(k * n, (k + 1) * n)
        total = 2.0 * nn(widen(lb_ref, m_ref, 0, n, 1 - k, rank), side[...])
        total = total + a_ref[rows].astype(F32) + b_ref[rows].astype(F32)
        own_ref[k * q : (k + 1) * q] = total[:q]
        left_ref[k * q : (k + 1) * q] = total[q : 2 * q]
        right_ref[k * q : (k + 1) * q] = total[2 * q : 3 * q]
        far = fd_ref if k == 0 else fu_ref
        far[...] = total[3 * q :].astype(BF)


def lift_body(rank, m_ref, lb_ref, own_ref, left_ref, right_ref, far_d_ref, far_u_ref, up_out, down_out):
    n = far_d_ref.shape[0]
    downs = [own_ref[:n], left_ref[:n], right_ref[:n], far_d_ref[...]]
    ups = [own_ref[n:], left_ref[n:], right_ref[n:], far_u_ref[...]]
    for which, blocks, out in ((0, ups, up_out), (1, downs, down_out)):
        total = None
        for g, block in enumerate(blocks):
            part = tn(widen(lb_ref, m_ref, g, n, which, rank), block)
            total = part if total is None else total + part
        out[...] = 2.0 * total


def swap_body(place_ref, w_ref, x_ref, out_ref):
    r = pl.program_id(0)

    @pl.when(r < 8)
    def _():
        out_ref[0] = w_ref[...]

    @pl.when(r == 8)
    def _():
        out_ref[0] = x_ref[...]


def for_other_core(w, x, places):
    n = x.shape[1]
    return pl.pallas_call(
        swap_body,
        grid_spec=pltpu.PrefetchScalarGridSpec(
            num_scalar_prefetch=1,
            grid=(9,),
            in_specs=[
                pl.BlockSpec((n, n), lambda r, s: (0, s[8 + jnp.minimum(r, 7)])),
                pl.BlockSpec((n, n), lambda r, s: (0, 0)),
            ],
            out_specs=pl.BlockSpec((1, n, n), lambda r, s: (r, 0, 0)),
        ),
        out_shape=jax.ShapeDtypeStruct((9, n, n), BF),
        compiler_params=pltpu.CompilerParams(vmem_limit_bytes=VMEM_LIMIT),
        cost_estimate=pl.CostEstimate(flops=0, bytes_accessed=18 * n * n * 2, transcendentals=0),
    )(places, w, x)


def with_weight(body, blocks, w, pair, places, ins, out, flops):
    n = w.shape[0]
    own = [pl.BlockSpec((n, n), lambda i, s, r=r: (0, s[r])) for r in blocks]
    other = [pl.BlockSpec((1, n, n), lambda i, s, r=r: (r, 0, 0)) for r in blocks]
    plain = [pl.BlockSpec(a.shape, lambda i, s, d=a.ndim: (0,) * d) for a in ins]
    k = len(blocks)

    def run(_, *refs):
        ws, vs = refs[:k], [v.at[0] for v in refs[k : 2 * k]]
        body(ws, vs, refs[2 * k : 2 * k + len(ins)], refs[2 * k + len(ins) :])

    size = 2 * k * n * n * 2 + sum(a.size * a.dtype.itemsize for a in (*ins, *out))
    return pl.pallas_call(
        run,
        grid_spec=pltpu.PrefetchScalarGridSpec(
            num_scalar_prefetch=1,
            grid=(1,),
            in_specs=own + other + plain,
            out_specs=[pl.BlockSpec(o.shape, lambda i, s: (0, 0)) for o in out],
        ),
        out_shape=out,
        compiler_params=pltpu.CompilerParams(vmem_limit_bytes=VMEM_LIMIT),
        cost_estimate=pl.CostEstimate(flops=flops, bytes_accessed=size, transcendentals=0),
    )(places, *([w] * k), *([pair] * k), *ins)


def two(x_ref, x2_ref, w, v):
    return nn(x_ref[...], w[...]) + nn(x2_ref[0], v[...])


def first_body(ws, vs, ins, outs):
    for w, v, out in zip(ws, vs, outs):
        out[...] = two(*ins, w, v).astype(BF)


def far_body(ws, vs, ins, outs):
    x, x2, from_z, from_left, from_right = ins
    far_a, far_b, z = outs
    h = far_a.shape[0]
    far = two(x, x2, ws[0], vs[0]) + from_z[...].astype(F32)
    far_a[...] = far[:h].astype(BF)
    far_b[...] = far[h:].astype(BF)
    z[...] = (
        two(x, x2, ws[1], vs[1]) + from_left[...].astype(F32) + from_right[...].astype(F32)
    ).astype(BF)


def near_body(ws, vs, ins, outs):
    x, x2, top, bottom = ins
    left, right = outs
    h = top.shape[0]
    a = two(x, x2, ws[0], vs[0])
    left[:h] = a[:h].astype(BF)
    left[h:] = (a[h:] + bottom[...].astype(F32)).astype(BF)
    b = two(x, x2, ws[1], vs[1])
    right[:h] = (b[:h] + top[...].astype(F32)).astype(BF)
    right[h:] = b[h:].astype(BF)


def last_body(ws, vs, ins, outs):
    x, x2, a, b, c, lifted = ins
    total = two(x, x2, ws[0], vs[0]) + lifted[...]
    total = total + a[...].astype(F32) + b[...].astype(F32) + c[...].astype(F32)
    outs[0][...] = total.astype(BF)


def back_near_body(ws, vs, ins, outs):
    own, left, right, far, z = (r[...] for r in ins)
    for out, w in zip(outs, (ws, vs)):
        total = nt(own, w[0][...]) + nt(left, w[1][...]) + nt(right, w[2][...])
        out[...] = total + nt(far, w[3][...]) + nt(z, w[4][...])


def back_other_body(ws, vs, ins, outs):
    a, b, c, near = (r[...] for r in ins)
    total = near + nt(a, vs[0][...]) + nt(b, vs[1][...]) + nt(c, vs[2][...])
    outs[0][...] = total.astype(BF)


def back_own_body(ws, vs, ins, outs):
    a, b, c, near, low, got = (r[...] for r in ins)
    total = near + low + nt(a, ws[0][...]) + nt(b, ws[1][...]) + nt(c, ws[2][...])
    outs[0][...] = (total + got.astype(F32)).astype(BF)


def adam_body(*refs):
    own, a, b = refs[:3]
    rows = own.shape[0] // 2
    ins, outs = refs[3:9], refs[9:]
    corr_one = 1.0 - 0.9**10
    corr_two = 1.0 - 0.999**10
    for k in range(2):
        at = slice(k * rows, (k + 1) * rows)
        grad = own[at] + a[at].astype(F32) + b[at].astype(F32)
        param = ins[3 * k][...]
        first = 0.9 * ins[3 * k + 1][...] + 0.1 * grad
        second = 0.999 * ins[3 * k + 2][...] + 0.001 * grad * grad
        step = first / corr_one / (jnp.sqrt(second / corr_two) + 1e-08)
        outs[3 * k][...] = param - 0.01 * (step + 0.1 * param)
        outs[3 * k + 1][...] = first
        outs[3 * k + 2][...] = second


def local(x, w, dy, counts, slots, down, up, down_m, down_v, up_m, up_v):
    toks, n = x.shape
    per, rank = up.shape[0], up.shape[1]
    flat = per * rank
    half = toks // 2
    dot = 2 * toks * n * n
    iy, iz, ix, il, ic = (lax.axis_index(a) for a in (*DP, *TENSOR))

    def down_rows(a):
        return jnp.transpose(a, (0, 2, 1)).reshape(flat, n)

    def up_rows(a):
        return a.reshape(flat, n)

    own_d, own_u = down_rows(down).astype(BF), up_rows(up).astype(BF)
    mine = jnp.concatenate([own_d, own_u], axis=0)
    z_left, z_right = send(mine, "zh", 1), send(mine, "zh", -1)
    d_left, d_right = send(dy, "x", 1), send(dy, "x", -1)
    d_z = send(dy, "zl", 1)

    columns = [((ix + s) % 4) * 4 + ((il + t) % 2) * 2 for t in (0, 1) for s in RING]
    places = jnp.stack([v + ic for v in columns] + [v + 1 - ic for v in columns]).astype(jnp.int32)
    pair = send(for_other_core(w, x, places), "c", 1)
    x2 = pair[8:9]
    mask = token_mask(slots, counts, jnp.stack([iy, iz]).astype(jnp.int32), rank, per, toks)

    z_far_d, z_far_u = send(z_left[:flat], "zh", 1), send(z_right[flat:], "zh", -1)
    group = jnp.concatenate(
        [own_d, z_left[:flat], z_right[:flat], z_far_d, own_u, z_left[flat:], z_right[flat:], z_far_u], axis=0
    )
    n4 = 4 * flat
    y_left, y_right = send(group, "y", 1), send(group, "y", -1)
    y_far_d, y_far_u = send(y_left[:n4], "y", 1), send(y_right[n4:], "y", -1)
    adapters = (group, y_left, y_right, y_far_d, y_far_u)

    lb = call(
        functools.partial(narrow_body, rank),
        [shape(2 * rank, toks, F32)],
        (x, dy, mask, *adapters),
        flops=4 * dot,
    )[0]
    lb = lb + send(lb, "c", 1)
    lb = lb + send(lb, "zl", 1)
    lb = lb + send(lb, "x", 1) + send(lb, "x", -1) + send(lb, "x", 2)

    fd, fu = call(
        functools.partial(grad_far_body, rank),
        [shape(n4, n, BF), shape(n4, n, BF)],
        (x, dy, mask, lb),
        flops=dot,
    )
    g_left, g_right = call(
        functools.partial(grad_near_body, rank),
        [shape(2 * n4, n, BF), shape(2 * n4, n, BF)],
        (x, dy, mask, lb, send(fd, "y", 1), send(fu, "y", -1)),
        flops=2 * dot,
    )
    fd, fu, g_left, g_right, g_own = call(
        functools.partial(grad_own_body, rank),
        [shape(flat, n, BF), shape(flat, n, BF)] + [shape(2 * flat, n, F32)] * 3,
        (x, dy, mask, lb, send(g_left, "y", -1), send(g_right, "y", 1)),
        flops=dot,
    )
    got_d, got_u = send(fd, "zh", 1).astype(F32), send(fu, "zh", -1).astype(F32)
    g_right = jnp.concatenate([g_right[:flat] + got_d, g_right[flat:]], axis=0).astype(BF)
    g_left = jnp.concatenate([g_left[:flat], g_left[flat:] + got_u], axis=0).astype(BF)
    from_left, from_right = send(g_right, "zh", 1), send(g_left, "zh", -1)
    new = call(
        adam_body,
        [shape(flat, n, F32)] * 6,
        (
            g_own,
            from_left,
            from_right,
            *(down_rows(a) for a in (down, down_m, down_v)),
            *(up_rows(a) for a in (up, up_m, up_v)),
        ),
    )
    new_down = [jnp.transpose(a.reshape(per, rank, n), (0, 2, 1)) for a in new[:3]]
    new_up = [a.reshape(per, rank, n) for a in new[3:]]

    lifted, low_grad = call(
        functools.partial(lift_body, rank),
        [shape(toks, n, F32), shape(toks, n, F32)],
        (mask, lb, *adapters),
        flops=4 * dot,
    )

    d_far = jnp.concatenate([send(d_left[:half], "x", 1), send(d_right[half:], "x", -1)], axis=0)
    d_zl, d_zr, d_zf = send(d_z, "x", 1), send(d_z, "x", -1), send(d_far, "zl", 1)

    block = shape(toks, n, BF)
    zl, zr, zf = with_weight(
        first_body, (5, 6, 7), w, pair, places, (x, x2), [block] * 3, 6 * dot
    )
    from_right, from_left, from_z = send(zl, "x", -1), send(zr, "x", 1), send(zf, "zl", 1)
    far_a, far_b, z = with_weight(
        far_body,
        (3, 4),
        w,
        pair,
        places,
        (x, x2, from_z, from_left, from_right),
        [shape(half, n, BF), shape(half, n, BF), block],
        4 * dot,
    )
    left, right = with_weight(
        near_body,
        (1, 2),
        w,
        pair,
        places,
        (x, x2, send(far_a, "x", 1), send(far_b, "x", -1)),
        [block] * 2,
        4 * dot,
    )
    proj_out = with_weight(
        last_body,
        (0,),
        w,
        pair,
        places,
        (x, x2, send(left, "x", -1), send(right, "x", 1), send(z, "zl", 1), lifted),
        [block],
        2 * dot,
    )[0]

    near_own, near_other = with_weight(
        back_near_body,
        (0, 1, 2, 3, 4),
        w,
        pair,
        places,
        (dy, d_left, d_right, d_far, d_z),
        [shape(toks, n, F32)] * 2,
        10 * dot,
    )
    other = with_weight(
        back_other_body, (5, 6, 7), w, pair, places, (d_zl, d_zr, d_zf, near_other), [block], 3 * dot
    )[0]
    input_grad = with_weight(
        back_own_body,
        (5, 6, 7),
        w,
        pair,
        places,
        (d_zl, d_zr, d_zf, near_own, low_grad, send(other, "c", 1)),
        [block],
        3 * dot,
    )[0]
    return (
        proj_out,
        input_grad,
        new_down[0],
        new_up[0],
        new_down[1],
        new_down[2],
        new_up[1],
        new_up[2],
    )


def solution(mesh):
    torus = Mesh(mesh.devices.reshape(4, 4, 4, 2, 2), (*DP, *TENSOR))
    return jax.shard_map(
        local,
        mesh=torus,
        in_specs=(
            P(DP, TENSOR),
            P(TENSOR, None),
            P(DP, TENSOR),
            P(DP, None),
            P(),
            P(DP, TENSOR, None),
            P(DP, None, TENSOR),
            P(DP, TENSOR, None),
            P(DP, TENSOR, None),
            P(DP, None, TENSOR),
            P(DP, None, TENSOR),
        ),
        out_specs=(
            P(DP, TENSOR),
            P(DP, TENSOR),
            P(DP, TENSOR, None),
            P(DP, None, TENSOR),
            P(DP, TENSOR, None),
            P(DP, TENSOR, None),
            P(DP, None, TENSOR),
            P(DP, None, TENSOR),
        ),
        check_vma=False,
    )
```

```python
import functools

import jax
import jax.numpy as jnp
from jax import lax
from jax.experimental import pallas as pl
from jax.experimental.pallas import tpu as pltpu
from jax.sharding import Mesh
from jax.sharding import PartitionSpec as P

DP = ("y", "zh")
TENSOR = ("x", "zl", "c")
BF = jnp.bfloat16
F32 = jnp.float32
RING = (0, 3, 1, 2)
VMEM_LIMIT = 16 * 1024 * 1024
WEIGHT_LIMIT = 46 * 1024 * 1024


def send(a, axis, step):
    n = lax.axis_size(axis)
    return lax.ppermute(a, axis, [(i, (i + step) % n) for i in range(n)])


def nn(a, b):
    return lax.dot_general(a, b, (((1,), (0,)), ((), ())), preferred_element_type=F32)


def nt(a, b):
    return lax.dot_general(a, b, (((1,), (1,)), ((), ())), preferred_element_type=F32)


def tn(a, b):
    return lax.dot_general(a, b, (((0,), (0,)), ((), ())), preferred_element_type=F32)


def call(body, out, ins, flops=0):
    size = sum(a.size * a.dtype.itemsize for a in ins) + sum(o.size * o.dtype.itemsize for o in out)
    return pl.pallas_call(
        body,
        out_shape=out,
        in_specs=[pl.BlockSpec(memory_space=pltpu.VMEM)] * len(ins),
        out_specs=[pl.BlockSpec(memory_space=pltpu.VMEM)] * len(out),
        compiler_params=pltpu.CompilerParams(vmem_limit_bytes=VMEM_LIMIT),
        cost_estimate=pl.CostEstimate(flops=flops, bytes_accessed=size, transcendentals=0),
    )(*ins)


def shape(rows, cols, dtype):
    return jax.ShapeDtypeStruct((rows, cols), dtype)


def mask_body(rank, per, slots_ref, counts_ref, place_ref, out_ref):
    rows, toks = out_ref.shape
    tenants = slots_ref.shape[1]
    row = lax.broadcasted_iota(jnp.int32, (rows, 1), 0)
    block = row // (rank * per)
    y = block // 4
    z = block - 4 * y
    ring_y = jnp.where(y == 1, 3, jnp.where(y == 2, 1, jnp.where(y == 3, 2, 0)))
    ring_z = jnp.where(z == 1, 3, jnp.where(z == 2, 1, jnp.where(z == 3, 2, 0)))
    at = ((place_ref[0] + ring_y) % 4) * 4 + (place_ref[1] + ring_z) % 4
    slot = at * per + (row // rank) % per
    lane = lax.broadcasted_iota(jnp.int32, (rows, tenants), 1).astype(F32)
    counts = counts_ref[...].astype(F32)
    hit = jnp.where(slots_ref[...] == slot, 1.0, 0.0)
    tenant = jnp.sum(hit * lane, axis=1, keepdims=True)
    first = jnp.sum(jnp.where(lane < tenant, counts, 0.0), axis=1, keepdims=True)
    last = first + jnp.sum(hit * counts, axis=1, keepdims=True)
    tok = lax.broadcasted_iota(jnp.int32, (1, toks), 1).astype(F32)
    for r in range(0, rows, 256):
        inside = (tok >= first[r : r + 256]) & (tok < last[r : r + 256])
        out_ref[r : r + 256] = jnp.where(inside, 1.0, 0.0).astype(BF)


def token_mask(slots, counts, place, rank, per, toks):
    rows = slots.shape[0] * rank
    return pl.pallas_call(
        functools.partial(mask_body, rank, per),
        out_shape=shape(rows, toks, BF),
        in_specs=[
            pl.BlockSpec(memory_space=pltpu.VMEM),
            pl.BlockSpec(memory_space=pltpu.VMEM),
            pl.BlockSpec(memory_space=pltpu.SMEM),
        ],
        out_specs=pl.BlockSpec(memory_space=pltpu.VMEM),
        compiler_params=pltpu.CompilerParams(vmem_limit_bytes=VMEM_LIMIT),
        cost_estimate=pl.CostEstimate(flops=0, bytes_accessed=rows * toks * 4, transcendentals=0),
    )(slots.reshape(1, -1), counts, place)


def narrow_body(rank, x_ref, dy_ref, m_ref, own_ref, left_ref, right_ref, far_d_ref, far_u_ref, out_ref):
    n = far_d_ref.shape[0]
    x, dy = x_ref[...], dy_ref[...]
    downs = [own_ref[:n], left_ref[:n], right_ref[:n], far_d_ref[...]]
    ups = [own_ref[n:], left_ref[n:], right_ref[n:], far_u_ref[...]]
    for k, (side, blocks) in enumerate(((x, downs), (dy, ups))):
        total = None
        for g, block in enumerate(blocks):
            wide = nt(block, side) * m_ref[g * n : (g + 1) * n].astype(F32)
            part = jnp.sum(wide.reshape(n // rank, rank, wide.shape[1]), axis=0)
            total = part if total is None else total + part
        out_ref[k * rank : (k + 1) * rank] = total


def widen(lb_ref, m_ref, g, n, which, rank):
    narrow = lb_ref[which * rank : (which + 1) * rank].astype(BF)
    return jnp.concatenate([narrow] * (n // rank), axis=0) * m_ref[g * n : (g + 1) * n]


def grad_far_body(rank, x_ref, dy_ref, m_ref, lb_ref, down_ref, up_ref):
    n = down_ref.shape[0]
    down_ref[...] = (2.0 * nn(widen(lb_ref, m_ref, 3, n, 1, rank), x_ref[...])).astype(BF)
    up_ref[...] = (2.0 * nn(widen(lb_ref, m_ref, 3, n, 0, rank), dy_ref[...])).astype(BF)


def grad_near_body(rank, x_ref, dy_ref, m_ref, lb_ref, got_down_ref, got_up_ref, left_ref, right_ref):
    n = got_down_ref.shape[0]
    x, dy = x_ref[...], dy_ref[...]
    left_ref[:n] = (2.0 * nn(widen(lb_ref, m_ref, 1, n, 1, rank), x)).astype(BF)
    left_ref[n:] = (
        2.0 * nn(widen(lb_ref, m_ref, 1, n, 0, rank), dy) + got_up_ref[...].astype(F32)
    ).astype(BF)
    right_ref[:n] = (
        2.0 * nn(widen(lb_ref, m_ref, 2, n, 1, rank), x) + got_down_ref[...].astype(F32)
    ).astype(BF)
    right_ref[n:] = (2.0 * nn(widen(lb_ref, m_ref, 2, n, 0, rank), dy)).astype(BF)


def grad_own_body(
    rank, x_ref, dy_ref, m_ref, lb_ref, a_ref, b_ref, far_ref, left_ref, right_ref, own_ref
):
    n = a_ref.shape[0] // 2
    q = n // 4
    for k, side in ((0, x_ref), (1, dy_ref)):
        rows = slice(k * n, (k + 1) * n)
        total = 2.0 * nn(widen(lb_ref, m_ref, 0, n, 1 - k, rank), side[...])
        total = total + a_ref[rows].astype(F32) + b_ref[rows].astype(F32)
        own_ref[k * q : (k + 1) * q] = total[:q]
        for i, ref in enumerate((left_ref, right_ref, far_ref)):
            ref[k * q : (k + 1) * q] = total[(i + 1) * q : (i + 2) * q].astype(BF)


def back_body(rank, get, ins, outs):
    x, x2, m_ref, lb_ref, own_ref, left_ref, right_ref, far_d_ref, far_u_ref, *parts = ins
    lifted, own_out, other_out = outs
    n = far_d_ref.shape[0]
    rows = x.shape[0]
    downs = [own_ref[:n], left_ref[:n], right_ref[:n], far_d_ref[...]]
    ups = [own_ref[n:], left_ref[n:], right_ref[n:], far_u_ref[...]]
    total = [None, None]
    for which, blocks in ((0, ups), (1, downs)):
        for g, block in enumerate(blocks):
            part = tn(widen(lb_ref, m_ref, g, n, which, rank), block)
            total[which] = part if g == 0 else total[which] + part
    w, v = get(0, 0), get(0, 1)
    lifted[...] = 2.0 * total[0] + nn(x[...], w) + nn(x2[...], v)
    first = parts[0][...]
    own = 2.0 * total[1] + nt(first, w)
    other = nt(first, v)
    for i in range(1, 8):
        part = parts[i][:rows]
        own = own + nt(part, get(i, 0))
        other = other + nt(part, get(i, 1))
    own_out[...] = own
    other_out[...] = other.astype(BF)


def with_weight(body, blocks, w, other, places, ins, out, flops):
    n = w.shape[0]
    k, m = len(blocks), len(ins)

    def run(place_ref, w_ref, v_ref, *refs):
        bufs, sems = refs[-2:]
        copies = {}
        for i, r in enumerate(blocks):
            at = pl.ds(pl.multiple_of(place_ref[r] * n, n), n)
            for j, src in enumerate((w_ref, v_ref)):
                copies[i, j] = pltpu.make_async_copy(src.at[:, at], bufs.at[i, j], sems.at[i, j])
                copies[i, j].start()

        def get(i, j):
            copies[i, j].wait()
            return bufs[i, j]

        body(get, refs[:m], refs[m:-2])

    size = 2 * k * n * n * 2 + sum(a.size * a.dtype.itemsize for a in (*ins, *out))
    return pl.pallas_call(
        run,
        in_specs=[pl.BlockSpec(memory_space=pltpu.SMEM)]
        + [pl.BlockSpec(memory_space=pltpu.HBM)] * 2
        + [pl.BlockSpec(memory_space=pltpu.VMEM)] * m,
        out_specs=[pl.BlockSpec(memory_space=pltpu.VMEM)] * len(out),
        out_shape=out,
        scratch_shapes=[pltpu.VMEM((k, 2, n, n), BF), pltpu.SemaphoreType.DMA((k, 2))],
        compiler_params=pltpu.CompilerParams(vmem_limit_bytes=WEIGHT_LIMIT),
        cost_estimate=pl.CostEstimate(flops=flops, bytes_accessed=size, transcendentals=0),
    )(places, w, other, *ins)


def two(x_ref, x2_ref, get, i):
    return nn(x_ref[...], get(i, 0)) + nn(x2_ref[...], get(i, 1))


def first_body(get, ins, outs):
    outs[0][...] = two(*ins, get, 0).astype(BF)


def far_body(get, ins, outs):
    x, x2, from_z = ins
    to_left, to_right = outs
    n = from_z.shape[0]
    h = n // 2
    far = two(x, x2, get, 0) + from_z[...].astype(F32)
    to_left[n:] = far[h:].astype(BF)
    to_right[n:] = far[:h].astype(BF)
    to_left[:n] = two(x, x2, get, 1).astype(BF)
    to_right[:n] = two(x, x2, get, 2).astype(BF)


def near_body(get, ins, outs):
    x, x2, from_left, from_right = ins
    left, right, z = outs
    n = left.shape[0]
    h = n // 2
    a = two(x, x2, get, 0)
    left[:h] = a[:h].astype(BF)
    left[h:] = (a[h:] + from_right[n:].astype(F32)).astype(BF)
    b = two(x, x2, get, 1)
    right[:h] = (b[:h] + from_left[n:].astype(F32)).astype(BF)
    right[h:] = b[h:].astype(BF)
    c = two(x, x2, get, 2)
    z[...] = (c + from_left[:n].astype(F32) + from_right[:n].astype(F32)).astype(BF)


def last_body(a, b, c, own, out):
    total = own[...] + a[...].astype(F32) + b[...].astype(F32) + c[...].astype(F32)
    out[...] = total.astype(BF)


def pack_body(z, left, right, to_left, to_right):
    n = z.shape[0]
    h = n // 2
    to_left[:n] = z[...]
    to_left[n:] = right[h:]
    to_right[:n] = z[...]
    to_right[n:] = left[:h]


def join_body(left, right, out):
    h = out.shape[0] // 2
    out[:h] = left[2 * h :]
    out[h:] = right[2 * h :]


def round_body(down, up, out):
    n = down.shape[0]
    out[:n] = down[...].astype(BF)
    out[n:] = up[...].astype(BF)


def group_body(own, left, right, far, out):
    n = own.shape[0] // 2
    for k in range(2):
        for i, a in enumerate((own, left, right, far)):
            out[(4 * k + i) * n : (4 * k + i + 1) * n] = a[k * n : (k + 1) * n]


def sum_body(a, b, out):
    out[...] = (a[...] + b[...].astype(F32)).astype(BF)


def adam_body(*refs):
    own, a, b, c = refs[:4]
    rows = own.shape[0] // 2
    ins, outs = refs[4:10], refs[10:]
    corr_one = 1.0 - 0.9**10
    corr_two = 1.0 - 0.999**10
    for k in range(2):
        at = slice(k * rows, (k + 1) * rows)
        grad = own[at] + a[at].astype(F32) + b[at].astype(F32) + c[at].astype(F32)
        param = ins[3 * k][...]
        first = 0.9 * ins[3 * k + 1][...] + 0.1 * grad
        second = 0.999 * ins[3 * k + 2][...] + 0.001 * grad * grad
        step = first / corr_one / (jnp.sqrt(second / corr_two) + 1e-08)
        outs[3 * k][...] = param - 0.01 * (step + 0.1 * param)
        outs[3 * k + 1][...] = first
        outs[3 * k + 2][...] = second


def tie(a, *before):
    return lax.optimization_barrier((a, *before))[0]


def local(x, w, dy, counts, slots, down, up, down_m, down_v, up_m, up_v):
    toks, n = x.shape
    per, rank = up.shape[0], up.shape[1]
    flat = per * rank
    n4 = 4 * flat
    half = toks // 2
    dot = 2 * toks * n * n
    block, wide = shape(toks, n, BF), shape(toks, n, F32)
    iy, iz, ix, il, ic = (lax.axis_index(a) for a in (*DP, *TENSOR))

    def down_rows(a):
        return jnp.transpose(a, (0, 2, 1)).reshape(flat, n)

    def up_rows(a):
        return a.reshape(flat, n)

    columns = [((ix + s) % 4) * 4 + ((il + t) % 2) * 2 + ic for t in (0, 1) for s in RING]
    places = jnp.stack(columns).astype(jnp.int32)

    pack = shape(toks + half, n, BF)

    def weighed(body, blocks, ins, out):
        return with_weight(body, blocks, w, other, places, ins, out, 2 * len(blocks) * dot)

    x2 = send(x, "c", 1)
    mine = call(round_body, [shape(2 * flat, n, BF)], (down_rows(down), up_rows(up)))[0]
    z_left, z_right, z_far = (send(tie(mine, x2), "zh", k) for k in (1, -1, 2))
    d_left, d_right = send(dy, "x", 1), send(dy, "x", -1)
    mask = token_mask(slots, counts, jnp.stack([iy, iz]).astype(jnp.int32), rank, per, toks)
    group = call(group_body, [shape(2 * n4, n, BF)], (tie(mine, mask), z_left, z_right, z_far))[0]
    y_left, y_right = send(group, "y", 1), send(group, "y", -1)
    other = send(tie(w, group), "c", 1)
    d_z = send(tie(dy, group), "zl", 1)
    to_left, to_right = call(pack_body, [pack] * 2, (d_z, d_left, d_right))
    y_far_d = send(y_left[:n4], "y", 1)
    y_far_u = send(y_right[n4:], "y", -1)
    a_left, a_right = send(to_right, "x", 1), send(to_left, "x", -1)
    zf = weighed(first_body, (7,), (x, x2), [block])[0]
    from_z = send(zf, "zl", 1)
    p_left, p_right = weighed(far_body, (3, 5, 6), (x, x2, from_z), [pack] * 2)
    adapters = (group, y_left, y_right, y_far_d, y_far_u)


    lb = call(
        functools.partial(narrow_body, rank),
        [shape(2 * rank, toks, F32)],
        (x, dy, tie(mask, p_left, a_left, a_right), *adapters),
        flops=4 * dot,
    )[0]
    lb = lb + send(lb, "c", 1)
    lb = lb + send(lb, "zl", 1)
    lb = lb + send(lb, "x", 1)
    lb = lb + send(lb, "x", 2)
    d_far = call(join_body, [block], (a_left, a_right))[0]

    fd, fu = call(
        functools.partial(grad_far_body, rank),
        [shape(n4, n, BF), shape(n4, n, BF)],
        (x, dy, mask, lb),
        flops=dot,
    )
    got_d, got_u = send(fd, "y", 1), send(fu, "y", -1)
    p_left, p_right, d_far_late = lax.optimization_barrier((p_left, p_right, d_far, lb))[:3]
    b_right, b_left = send(p_left, "x", -1), send(p_right, "x", 1)
    d_zf = send(d_far_late, "zl", 1)
    g_left, g_right = call(
        functools.partial(grad_near_body, rank),
        [shape(2 * n4, n, BF), shape(2 * n4, n, BF)],
        (x, dy, mask, lb, got_d, got_u),
        flops=2 * dot,
    )
    got_l, got_r = send(g_left, "y", -1), send(g_right, "y", 1)
    left, right, z = weighed(near_body, (1, 2, 4), (x, x2, tie(b_left, d_zf), b_right), [block] * 3)
    sums = (send(left, "x", -1), send(right, "x", 1), send(z, "zl", 1))
    lifted, own_grad, to_other = weighed(
        functools.partial(back_body, rank),
        tuple(range(8)),
        (
            x,
            x2,
            mask,
            lb,
            *adapters,
            tie(dy, left),
            d_left,
            d_right,
            d_far,
            d_z,
            a_left,
            a_right,
            d_zf,
        ),
        [wide, wide, block],
    )
    from_other = send(to_other, "c", 1)
    g_far, g_left, g_right, g_own = call(
        functools.partial(grad_own_body, rank),
        [shape(2 * flat, n, BF)] * 3 + [shape(2 * flat, n, F32)],
        (x, dy, mask, lb, tie(got_l, *sums, lifted), got_r),
        flops=dot,
    )
    from_far = send(g_far, "zh", 2)
    from_left, from_right = send(g_right, "zh", 1), send(g_left, "zh", -1)
    input_grad = call(sum_body, [block], (tie(own_grad, g_far), from_other))[0]

    new = call(
        adam_body,
        [shape(flat, n, F32)] * 6,
        (
            g_own,
            from_left,
            from_right,
            from_far,
            *(down_rows(a) for a in (down, down_m, down_v)),
            *(up_rows(a) for a in (up, up_m, up_v)),
        ),
    )
    new_down = [jnp.transpose(a.reshape(per, rank, n), (0, 2, 1)) for a in new[:3]]
    new_up = [a.reshape(per, rank, n) for a in new[3:]]
    proj_out = call(last_body, [block], (*sums, lifted))[0]
    return (
        proj_out,
        input_grad,
        new_down[0],
        new_up[0],
        new_down[1],
        new_down[2],
        new_up[1],
        new_up[2],
    )


def solution(mesh):
    torus = Mesh(mesh.devices.reshape(4, 4, 4, 2, 2), (*DP, *TENSOR))
    return jax.shard_map(
        local,
        mesh=torus,
        in_specs=(
            P(DP, TENSOR),
            P(TENSOR, None),
            P(DP, TENSOR),
            P(DP, None),
            P(),
            P(DP, TENSOR, None),
            P(DP, None, TENSOR),
            P(DP, TENSOR, None),
            P(DP, TENSOR, None),
            P(DP, None, TENSOR),
            P(DP, None, TENSOR),
        ),
        out_specs=(
            P(DP, TENSOR),
            P(DP, TENSOR),
            P(DP, TENSOR, None),
            P(DP, None, TENSOR),
            P(DP, TENSOR, None),
            P(DP, TENSOR, None),
            P(DP, None, TENSOR),
            P(DP, None, TENSOR),
        ),
        check_vma=False,
    )
```

```python
import functools

import jax
import jax.numpy as jnp
from jax import lax
from jax.experimental import pallas as pl
from jax.experimental.pallas import tpu as pltpu
from jax.sharding import Mesh
from jax.sharding import PartitionSpec as P

DP = ("y", "zh")
TENSOR = ("x", "zl", "c")
BF = jnp.bfloat16
F32 = jnp.float32
RING = (0, 3, 1, 2)
VMEM_LIMIT = 16 * 1024 * 1024
WEIGHT_LIMIT = 46 * 1024 * 1024


def send(a, axis, step):
    n = lax.axis_size(axis)
    return lax.ppermute(a, axis, [(i, (i + step) % n) for i in range(n)])


def nn(a, b):
    return lax.dot_general(a, b, (((1,), (0,)), ((), ())), preferred_element_type=F32)


def nt(a, b):
    return lax.dot_general(a, b, (((1,), (1,)), ((), ())), preferred_element_type=F32)


def tn(a, b):
    return lax.dot_general(a, b, (((0,), (0,)), ((), ())), preferred_element_type=F32)


def call(body, out, ins, flops=0):
    size = sum(a.size * a.dtype.itemsize for a in ins) + sum(o.size * o.dtype.itemsize for o in out)
    return pl.pallas_call(
        body,
        out_shape=out,
        in_specs=[pl.BlockSpec(memory_space=pltpu.VMEM)] * len(ins),
        out_specs=[pl.BlockSpec(memory_space=pltpu.VMEM)] * len(out),
        compiler_params=pltpu.CompilerParams(vmem_limit_bytes=VMEM_LIMIT),
        cost_estimate=pl.CostEstimate(flops=flops, bytes_accessed=size, transcendentals=0),
    )(*ins)


def shape(rows, cols, dtype):
    return jax.ShapeDtypeStruct((rows, cols), dtype)


def mask_body(rank, per, slots_ref, counts_ref, place_ref, out_ref):
    rows, toks = out_ref.shape
    tenants = slots_ref.shape[1]
    row = lax.broadcasted_iota(jnp.int32, (rows, 1), 0)
    block = row // (rank * per)
    y = block // 4
    z = block - 4 * y
    ring_y = jnp.where(y == 1, 3, jnp.where(y == 2, 1, jnp.where(y == 3, 2, 0)))
    ring_z = jnp.where(z == 1, 3, jnp.where(z == 2, 1, jnp.where(z == 3, 2, 0)))
    at = ((place_ref[0] + ring_y) % 4) * 4 + (place_ref[1] + ring_z) % 4
    slot = at * per + (row // rank) % per
    lane = lax.broadcasted_iota(jnp.int32, (rows, tenants), 1).astype(F32)
    counts = counts_ref[...].astype(F32)
    hit = jnp.where(slots_ref[...] == slot, 1.0, 0.0)
    tenant = jnp.sum(hit * lane, axis=1, keepdims=True)
    first = jnp.sum(jnp.where(lane < tenant, counts, 0.0), axis=1, keepdims=True)
    last = first + jnp.sum(hit * counts, axis=1, keepdims=True)
    tok = lax.broadcasted_iota(jnp.int32, (1, toks), 1).astype(F32)
    for r in range(0, rows, 256):
        inside = (tok >= first[r : r + 256]) & (tok < last[r : r + 256])
        out_ref[r : r + 256] = jnp.where(inside, 1.0, 0.0).astype(BF)


def token_mask(slots, counts, place, rank, per, toks):
    rows = slots.shape[0] * rank
    return pl.pallas_call(
        functools.partial(mask_body, rank, per),
        out_shape=shape(rows, toks, BF),
        in_specs=[
            pl.BlockSpec(memory_space=pltpu.VMEM),
            pl.BlockSpec(memory_space=pltpu.VMEM),
            pl.BlockSpec(memory_space=pltpu.SMEM),
        ],
        out_specs=pl.BlockSpec(memory_space=pltpu.VMEM),
        compiler_params=pltpu.CompilerParams(vmem_limit_bytes=VMEM_LIMIT),
        cost_estimate=pl.CostEstimate(flops=0, bytes_accessed=rows * toks * 4, transcendentals=0),
    )(slots.reshape(1, -1), counts, place)


def narrow_body(rank, x_ref, dy_ref, m_ref, own_ref, left_ref, right_ref, far_d_ref, far_u_ref, out_ref):
    n = far_d_ref.shape[0]
    x, dy = x_ref[...], dy_ref[...]
    downs = [own_ref[:n], left_ref[:n], right_ref[:n], far_d_ref[...]]
    ups = [own_ref[n:], left_ref[n:], right_ref[n:], far_u_ref[...]]
    for k, (side, blocks) in enumerate(((x, downs), (dy, ups))):
        total = None
        for g, block in enumerate(blocks):
            wide = nt(block, side) * m_ref[g * n : (g + 1) * n].astype(F32)
            part = jnp.sum(wide.reshape(n // rank, rank, wide.shape[1]), axis=0)
            total = part if total is None else total + part
        out_ref[k * rank : (k + 1) * rank] = total


def widen(lb_ref, m_ref, g, n, which, rank):
    narrow = lb_ref[which * rank : (which + 1) * rank].astype(BF)
    return jnp.concatenate([narrow] * (n // rank), axis=0) * m_ref[g * n : (g + 1) * n]


def grad_far_body(rank, x_ref, dy_ref, m_ref, lb_ref, down_ref, up_ref):
    n = down_ref.shape[0]
    down_ref[...] = (2.0 * nn(widen(lb_ref, m_ref, 3, n, 1, rank), x_ref[...])).astype(BF)
    up_ref[...] = (2.0 * nn(widen(lb_ref, m_ref, 3, n, 0, rank), dy_ref[...])).astype(BF)


def grad_near_body(rank, x_ref, dy_ref, m_ref, lb_ref, got_down_ref, got_up_ref, left_ref, right_ref):
    n = got_down_ref.shape[0]
    x, dy = x_ref[...], dy_ref[...]
    left_ref[:n] = (2.0 * nn(widen(lb_ref, m_ref, 1, n, 1, rank), x)).astype(BF)
    left_ref[n:] = (
        2.0 * nn(widen(lb_ref, m_ref, 1, n, 0, rank), dy) + got_up_ref[...].astype(F32)
    ).astype(BF)
    right_ref[:n] = (
        2.0 * nn(widen(lb_ref, m_ref, 2, n, 1, rank), x) + got_down_ref[...].astype(F32)
    ).astype(BF)
    right_ref[n:] = (2.0 * nn(widen(lb_ref, m_ref, 2, n, 0, rank), dy)).astype(BF)


def grad_own_body(
    rank, x_ref, dy_ref, m_ref, lb_ref, a_ref, b_ref, far_ref, left_ref, right_ref, own_ref
):
    n = a_ref.shape[0] // 2
    q = n // 4
    for k, side in ((0, x_ref), (1, dy_ref)):
        rows = slice(k * n, (k + 1) * n)
        total = 2.0 * nn(widen(lb_ref, m_ref, 0, n, 1 - k, rank), side[...])
        total = total + a_ref[rows].astype(F32) + b_ref[rows].astype(F32)
        own_ref[k * q : (k + 1) * q] = total[:q]
        for i, ref in enumerate((left_ref, right_ref, far_ref)):
            ref[k * q : (k + 1) * q] = total[(i + 1) * q : (i + 2) * q].astype(BF)


def back_body(rank, get, ins, outs):
    x, x2, m_ref, lb_ref, own_ref, left_ref, right_ref, far_d_ref, far_u_ref, *parts = ins
    lifted, own_out, other_out = outs
    n = far_d_ref.shape[0]
    downs = [own_ref[:n], left_ref[:n], right_ref[:n], far_d_ref[...]]
    ups = [own_ref[n:], left_ref[n:], right_ref[n:], far_u_ref[...]]
    total = [None, None]
    for which, blocks in ((0, ups), (1, downs)):
        for g, block in enumerate(blocks):
            part = tn(widen(lb_ref, m_ref, g, n, which, rank), block)
            total[which] = part if g == 0 else total[which] + part
    w, v = get(0, 0), get(0, 1)
    lifted[...] = 2.0 * total[0] + nn(x[...], w) + nn(x2[...], v)
    part, own, other = parts
    own_out[...] = 2.0 * total[1] + own[...] + nt(part[...], get(1, 0))
    other_out[...] = (other[...] + nt(part[...], get(1, 1))).astype(BF)


def with_weight(body, blocks, w, other, places, ins, out, flops):
    n = w.shape[0]
    k, m = len(blocks), len(ins)

    def run(place_ref, w_ref, v_ref, *refs):
        bufs, sems = refs[-2:]
        copies = {}
        for i, r in enumerate(blocks):
            at = pl.ds(pl.multiple_of(place_ref[r] * n, n), n)
            for j, src in enumerate((w_ref, v_ref)):
                copies[i, j] = pltpu.make_async_copy(src.at[:, at], bufs.at[i, j], sems.at[i, j])
                copies[i, j].start()

        def get(i, j):
            copies[i, j].wait()
            return bufs[i, j]

        body(get, refs[:m], refs[m:-2])

    size = 2 * k * n * n * 2 + sum(a.size * a.dtype.itemsize for a in (*ins, *out))
    return pl.pallas_call(
        run,
        in_specs=[pl.BlockSpec(memory_space=pltpu.SMEM)]
        + [pl.BlockSpec(memory_space=pltpu.HBM)] * 2
        + [pl.BlockSpec(memory_space=pltpu.VMEM)] * m,
        out_specs=[pl.BlockSpec(memory_space=pltpu.VMEM)] * len(out),
        out_shape=out,
        scratch_shapes=[pltpu.VMEM((k, 2, n, n), BF), pltpu.SemaphoreType.DMA((k, 2))],
        compiler_params=pltpu.CompilerParams(vmem_limit_bytes=WEIGHT_LIMIT),
        cost_estimate=pl.CostEstimate(flops=flops, bytes_accessed=size, transcendentals=0),
    )(places, w, other, *ins)


def two(x_ref, x2_ref, get, i):
    return nn(x_ref[...], get(i, 0)) + nn(x2_ref[...], get(i, 1))


def first_body(get, ins, outs):
    outs[0][...] = two(*ins, get, 0).astype(BF)


def far_body(get, ins, outs):
    x, x2, from_z = ins
    to_left, to_right = outs
    n = from_z.shape[0]
    h = n // 2
    far = two(x, x2, get, 0) + from_z[...].astype(F32)
    to_left[n:] = far[h:].astype(BF)
    to_right[n:] = far[:h].astype(BF)
    to_left[:n] = two(x, x2, get, 1).astype(BF)
    to_right[:n] = two(x, x2, get, 2).astype(BF)


def near_body(get, ins, outs):
    x, x2, from_left, from_right = ins
    left, right, z = outs
    n = left.shape[0]
    h = n // 2
    a = two(x, x2, get, 0)
    left[:h] = a[:h].astype(BF)
    left[h:] = (a[h:] + from_right[n:].astype(F32)).astype(BF)
    b = two(x, x2, get, 1)
    right[:h] = (b[:h] + from_left[n:].astype(F32)).astype(BF)
    right[h:] = b[h:].astype(BF)
    c = two(x, x2, get, 2)
    z[...] = (c + from_left[:n].astype(F32) + from_right[:n].astype(F32)).astype(BF)


def last_body(a, b, c, own, out):
    total = own[...] + a[...].astype(F32) + b[...].astype(F32) + c[...].astype(F32)
    out[...] = total.astype(BF)


def back_near_body(get, ins, outs):
    total = [None, None]
    for i, part in enumerate(ins):
        for j in range(2):
            more = nt(part[...], get(i, j))
            total[j] = more if total[j] is None else total[j] + more
    for out, t in zip(outs, total):
        out[...] = t


def back_more_body(get, ins, outs):
    *parts, own, other = ins
    total = [own[...], other[...]]
    for i, part in enumerate(parts):
        rows = own.shape[0]
        for j in range(2):
            total[j] = total[j] + nt(part[:rows], get(i, j))
    for out, t in zip(outs, total):
        out[...] = t


def pack_body(z, left, right, to_left, to_right):
    n = z.shape[0]
    h = n // 2
    to_left[:n] = z[...]
    to_left[n:] = right[h:]
    to_right[:n] = z[...]
    to_right[n:] = left[:h]


def join_body(left, right, out):
    h = out.shape[0] // 2
    out[:h] = left[2 * h :]
    out[h:] = right[2 * h :]


def round_body(down, up, out):
    n = down.shape[0]
    out[:n] = down[...].astype(BF)
    out[n:] = up[...].astype(BF)


def group_body(own, left, right, far, out):
    n = own.shape[0] // 2
    for k in range(2):
        for i, a in enumerate((own, left, right, far)):
            out[(4 * k + i) * n : (4 * k + i + 1) * n] = a[k * n : (k + 1) * n]


def sum_body(a, b, out):
    out[...] = (a[...] + b[...].astype(F32)).astype(BF)


def adam_body(*refs):
    own, a, b, c = refs[:4]
    rows = own.shape[0] // 2
    ins, outs = refs[4:10], refs[10:]
    corr_one = 1.0 - 0.9**10
    corr_two = 1.0 - 0.999**10
    for k in range(2):
        at = slice(k * rows, (k + 1) * rows)
        grad = own[at] + a[at].astype(F32) + b[at].astype(F32) + c[at].astype(F32)
        param = ins[3 * k][...]
        first = 0.9 * ins[3 * k + 1][...] + 0.1 * grad
        second = 0.999 * ins[3 * k + 2][...] + 0.001 * grad * grad
        step = first / corr_one / (jnp.sqrt(second / corr_two) + 1e-08)
        outs[3 * k][...] = param - 0.01 * (step + 0.1 * param)
        outs[3 * k + 1][...] = first
        outs[3 * k + 2][...] = second


def tie(a, *before):
    return lax.optimization_barrier((a, *before))[0]


def local(x, w, dy, counts, slots, down, up, down_m, down_v, up_m, up_v):
    toks, n = x.shape
    per, rank = up.shape[0], up.shape[1]
    flat = per * rank
    n4 = 4 * flat
    half = toks // 2
    dot = 2 * toks * n * n
    block, wide = shape(toks, n, BF), shape(toks, n, F32)
    iy, iz, ix, il, ic = (lax.axis_index(a) for a in (*DP, *TENSOR))

    def down_rows(a):
        return jnp.transpose(a, (0, 2, 1)).reshape(flat, n)

    def up_rows(a):
        return a.reshape(flat, n)

    columns = [((ix + s) % 4) * 4 + ((il + t) % 2) * 2 + ic for t in (0, 1) for s in RING]
    places = jnp.stack(columns).astype(jnp.int32)

    pack = shape(toks + half, n, BF)

    def weighed(body, blocks, ins, out):
        return with_weight(body, blocks, w, other, places, ins, out, 2 * len(blocks) * dot)

    x2 = send(x, "c", 1)
    mine = call(round_body, [shape(2 * flat, n, BF)], (down_rows(down), up_rows(up)))[0]
    z_left, z_right, z_far = (send(tie(mine, x2), "zh", k) for k in (1, -1, 2))
    d_left, d_right = send(dy, "x", 1), send(dy, "x", -1)
    mask = token_mask(slots, counts, jnp.stack([iy, iz]).astype(jnp.int32), rank, per, toks)
    group = call(group_body, [shape(2 * n4, n, BF)], (tie(mine, mask), z_left, z_right, z_far))[0]
    y_left, y_right = send(group, "y", 1), send(group, "y", -1)
    other = send(tie(w, group, d_left, d_right), "c", 1)
    d_z = send(tie(dy, group), "zl", 1)
    zf = weighed(first_body, (7,), (x, x2), [block])[0]
    to_left, to_right = call(pack_body, [pack] * 2, (tie(d_z, y_left, y_right, zf), d_left, d_right))
    a_left, a_right = send(to_right, "x", 1), send(to_left, "x", -1)
    y_far_d = send(y_left[:n4], "y", 1)
    y_far_u = send(y_right[n4:], "y", -1)
    from_z = send(zf, "zl", 1)
    p_left, p_right = weighed(far_body, (3, 5, 6), (x, x2, tie(from_z, y_far_d, y_far_u)), [pack] * 2)
    adapters = (group, y_left, y_right, y_far_d, y_far_u)


    lb = call(
        functools.partial(narrow_body, rank),
        [shape(2 * rank, toks, F32)],
        (x, dy, tie(mask, p_left), *adapters),
        flops=4 * dot,
    )[0]
    lb = lb + send(lb, "c", 1)
    lb = tie(lb + send(lb, "zl", 1), a_left, a_right)
    near = weighed(back_near_body, (0, 1, 2, 4), (tie(dy, lb), d_left, d_right, d_z), [wide] * 2)
    lb = tie(lb, *near) + send(lb, "x", 1)
    d_far = call(join_body, [block], (tie(a_left, lb), a_right))[0]
    near = weighed(back_more_body, (3, 5, 6), (d_far, a_left, a_right, *near), [wide] * 2)
    lb = tie(lb, *near) + send(lb, "x", 2)

    fd, fu = call(
        functools.partial(grad_far_body, rank),
        [shape(n4, n, BF), shape(n4, n, BF)],
        (x, dy, mask, lb),
        flops=dot,
    )
    got_d, got_u = send(fd, "y", 1), send(fu, "y", -1)
    p_left, p_right, d_far_late = lax.optimization_barrier((p_left, p_right, d_far, lb))[:3]
    b_right, b_left = send(p_left, "x", -1), send(p_right, "x", 1)
    d_zf = send(d_far_late, "zl", 1)
    g_left, g_right = call(
        functools.partial(grad_near_body, rank),
        [shape(2 * n4, n, BF), shape(2 * n4, n, BF)],
        (x, dy, mask, lb, got_d, got_u),
        flops=2 * dot,
    )
    got_l, got_r = send(g_left, "y", -1), send(g_right, "y", 1)
    left, right, z = weighed(near_body, (1, 2, 4), (x, x2, tie(b_left, d_zf), b_right), [block] * 3)
    left, right, z = lax.optimization_barrier((left, right, z, got_l, got_r))[:3]
    sums = (send(left, "x", -1), send(right, "x", 1), send(z, "zl", 1))
    lifted, own_grad, to_other = weighed(
        functools.partial(back_body, rank),
        (0, 7),
        (
            x,
            x2,
            mask,
            lb,
            *adapters,
            tie(d_zf, left),
            *near,
        ),
        [wide, wide, block],
    )
    from_other = send(to_other, "c", 1)
    g_far, g_left, g_right, g_own = call(
        functools.partial(grad_own_body, rank),
        [shape(2 * flat, n, BF)] * 3 + [shape(2 * flat, n, F32)],
        (x, dy, mask, lb, tie(got_l, *sums, lifted), got_r),
        flops=dot,
    )
    from_far = send(g_far, "zh", 2)
    from_left, from_right = send(g_right, "zh", 1), send(g_left, "zh", -1)
    input_grad = call(sum_body, [block], (tie(own_grad, g_far), from_other))[0]

    new = call(
        adam_body,
        [shape(flat, n, F32)] * 6,
        (
            g_own,
            from_left,
            from_right,
            from_far,
            *(down_rows(a) for a in (down, down_m, down_v)),
            *(up_rows(a) for a in (up, up_m, up_v)),
        ),
    )
    new_down = [jnp.transpose(a.reshape(per, rank, n), (0, 2, 1)) for a in new[:3]]
    new_up = [a.reshape(per, rank, n) for a in new[3:]]
    proj_out = call(last_body, [block], (*sums, lifted))[0]
    return (
        proj_out,
        input_grad,
        new_down[0],
        new_up[0],
        new_down[1],
        new_down[2],
        new_up[1],
        new_up[2],
    )


def solution(mesh):
    torus = Mesh(mesh.devices.reshape(4, 4, 4, 2, 2), (*DP, *TENSOR))
    return jax.shard_map(
        local,
        mesh=torus,
        in_specs=(
            P(DP, TENSOR),
            P(TENSOR, None),
            P(DP, TENSOR),
            P(DP, None),
            P(),
            P(DP, TENSOR, None),
            P(DP, None, TENSOR),
            P(DP, TENSOR, None),
            P(DP, TENSOR, None),
            P(DP, None, TENSOR),
            P(DP, None, TENSOR),
        ),
        out_specs=(
            P(DP, TENSOR),
            P(DP, TENSOR),
            P(DP, TENSOR, None),
            P(DP, None, TENSOR),
            P(DP, TENSOR, None),
            P(DP, TENSOR, None),
            P(DP, None, TENSOR),
            P(DP, None, TENSOR),
        ),
        check_vma=False,
    )
```

```python
import functools

import jax
import jax.numpy as jnp
from jax import lax
from jax.experimental import pallas as pl
from jax.experimental.pallas import tpu as pltpu
from jax.sharding import Mesh
from jax.sharding import PartitionSpec as P

DP = ("y", "zh")
TENSOR = ("x", "zl", "c")
BF = jnp.bfloat16
F32 = jnp.float32
RING = (0, 3, 1, 2)
VMEM_LIMIT = 16 * 1024 * 1024
WEIGHT_LIMIT = 46 * 1024 * 1024


def send(a, axis, step):
    n = lax.axis_size(axis)
    return lax.ppermute(a, axis, [(i, (i + step) % n) for i in range(n)])


def nn(a, b):
    return lax.dot_general(a, b, (((1,), (0,)), ((), ())), preferred_element_type=F32)


def nt(a, b):
    return lax.dot_general(a, b, (((1,), (1,)), ((), ())), preferred_element_type=F32)


def tn(a, b):
    return lax.dot_general(a, b, (((0,), (0,)), ((), ())), preferred_element_type=F32)


def call(body, out, ins, flops=0):
    size = sum(a.size * a.dtype.itemsize for a in ins) + sum(o.size * o.dtype.itemsize for o in out)
    return pl.pallas_call(
        body,
        out_shape=out,
        in_specs=[pl.BlockSpec(memory_space=pltpu.VMEM)] * len(ins),
        out_specs=[pl.BlockSpec(memory_space=pltpu.VMEM)] * len(out),
        compiler_params=pltpu.CompilerParams(vmem_limit_bytes=VMEM_LIMIT),
        cost_estimate=pl.CostEstimate(flops=flops, bytes_accessed=size, transcendentals=0),
    )(*ins)


def shape(rows, cols, dtype):
    return jax.ShapeDtypeStruct((rows, cols), dtype)


def mask_body(rank, per, slots_ref, counts_ref, place_ref, out_ref):
    rows, toks = out_ref.shape
    tenants = slots_ref.shape[1]
    row = lax.broadcasted_iota(jnp.int32, (rows, 1), 0)
    block = row // (rank * per)
    y = block // 4
    z = block - 4 * y
    ring_y = jnp.where(y == 1, 3, jnp.where(y == 2, 1, jnp.where(y == 3, 2, 0)))
    ring_z = jnp.where(z == 1, 3, jnp.where(z == 2, 1, jnp.where(z == 3, 2, 0)))
    at = ((place_ref[0] + ring_y) % 4) * 4 + (place_ref[1] + ring_z) % 4
    slot = at * per + (row // rank) % per
    lane = lax.broadcasted_iota(jnp.int32, (rows, tenants), 1).astype(F32)
    counts = counts_ref[...].astype(F32)
    hit = jnp.where(slots_ref[...] == slot, 1.0, 0.0)
    tenant = jnp.sum(hit * lane, axis=1, keepdims=True)
    first = jnp.sum(jnp.where(lane < tenant, counts, 0.0), axis=1, keepdims=True)
    last = first + jnp.sum(hit * counts, axis=1, keepdims=True)
    tok = lax.broadcasted_iota(jnp.int32, (1, toks), 1).astype(F32)
    for r in range(0, rows, 256):
        inside = (tok >= first[r : r + 256]) & (tok < last[r : r + 256])
        out_ref[r : r + 256] = jnp.where(inside, 1.0, 0.0).astype(BF)


def token_mask(slots, counts, place, rank, per, toks):
    rows = slots.shape[0] * rank
    return pl.pallas_call(
        functools.partial(mask_body, rank, per),
        out_shape=shape(rows, toks, BF),
        in_specs=[
            pl.BlockSpec(memory_space=pltpu.VMEM),
            pl.BlockSpec(memory_space=pltpu.VMEM),
            pl.BlockSpec(memory_space=pltpu.SMEM),
        ],
        out_specs=pl.BlockSpec(memory_space=pltpu.VMEM),
        compiler_params=pltpu.CompilerParams(vmem_limit_bytes=VMEM_LIMIT),
        cost_estimate=pl.CostEstimate(flops=0, bytes_accessed=rows * toks * 4, transcendentals=0),
    )(slots.reshape(1, -1), counts, place)


def narrow_body(rank, x_ref, dy_ref, m_ref, own_ref, left_ref, right_ref, far_d_ref, far_u_ref, out_ref):
    n = far_d_ref.shape[0]
    x, dy = x_ref[...], dy_ref[...]
    downs = [own_ref[:n], left_ref[:n], right_ref[:n], far_d_ref[...]]
    ups = [own_ref[n:], left_ref[n:], right_ref[n:], far_u_ref[...]]
    for k, (side, blocks) in enumerate(((x, downs), (dy, ups))):
        total = None
        for g, block in enumerate(blocks):
            wide = nt(block, side) * m_ref[g * n : (g + 1) * n].astype(F32)
            part = jnp.sum(wide.reshape(n // rank, rank, wide.shape[1]), axis=0)
            total = part if total is None else total + part
        out_ref[k * rank : (k + 1) * rank] = total


def widen(lb_ref, m_ref, g, n, which, rank):
    narrow = lb_ref[which * rank : (which + 1) * rank].astype(BF)
    return jnp.concatenate([narrow] * (n // rank), axis=0) * m_ref[g * n : (g + 1) * n]


def grad_far_body(rank, x_ref, dy_ref, m_ref, lb_ref, down_ref, up_ref):
    n = down_ref.shape[0]
    down_ref[...] = (2.0 * nn(widen(lb_ref, m_ref, 3, n, 1, rank), x_ref[...])).astype(BF)
    up_ref[...] = (2.0 * nn(widen(lb_ref, m_ref, 3, n, 0, rank), dy_ref[...])).astype(BF)


def grad_near_body(rank, x_ref, dy_ref, m_ref, lb_ref, got_down_ref, got_up_ref, left_ref, right_ref):
    n = got_down_ref.shape[0]
    x, dy = x_ref[...], dy_ref[...]
    left_ref[:n] = (2.0 * nn(widen(lb_ref, m_ref, 1, n, 1, rank), x)).astype(BF)
    left_ref[n:] = (
        2.0 * nn(widen(lb_ref, m_ref, 1, n, 0, rank), dy) + got_up_ref[...].astype(F32)
    ).astype(BF)
    right_ref[:n] = (
        2.0 * nn(widen(lb_ref, m_ref, 2, n, 1, rank), x) + got_down_ref[...].astype(F32)
    ).astype(BF)
    right_ref[n:] = (2.0 * nn(widen(lb_ref, m_ref, 2, n, 0, rank), dy)).astype(BF)


def grad_own_body(
    rank, x_ref, dy_ref, m_ref, lb_ref, a_ref, b_ref, far_ref, left_ref, right_ref, own_ref
):
    n = a_ref.shape[0] // 2
    q = n // 4
    for k, side in ((0, x_ref), (1, dy_ref)):
        rows = slice(k * n, (k + 1) * n)
        total = 2.0 * nn(widen(lb_ref, m_ref, 0, n, 1 - k, rank), side[...])
        total = total + a_ref[rows].astype(F32) + b_ref[rows].astype(F32)
        own_ref[k * q : (k + 1) * q] = total[:q]
        for i, ref in enumerate((left_ref, right_ref, far_ref)):
            ref[k * q : (k + 1) * q] = total[(i + 1) * q : (i + 2) * q].astype(BF)


def back_body(rank, get, ins, outs):
    x, x2, m_ref, lb_ref, own_ref, left_ref, right_ref, far_d_ref, far_u_ref, *parts = ins
    lifted, own_out, other_out = outs
    n = far_d_ref.shape[0]
    downs = [own_ref[:n], left_ref[:n], right_ref[:n], far_d_ref[...]]
    ups = [own_ref[n:], left_ref[n:], right_ref[n:], far_u_ref[...]]
    total = [None, None]
    for which, blocks in ((0, ups), (1, downs)):
        for g, block in enumerate(blocks):
            part = tn(widen(lb_ref, m_ref, g, n, which, rank), block)
            total[which] = part if g == 0 else total[which] + part
    w, v = get(0, 0), get(0, 1)
    lifted[...] = 2.0 * total[0] + nn(x[...], w) + nn(x2[...], v)
    part, own, other = parts
    own_out[...] = 2.0 * total[1] + own[...] + nt(part[...], get(1, 0))
    other_out[...] = (other[...] + nt(part[...], get(1, 1))).astype(BF)


def with_weight(body, blocks, w, other, places, ins, out, flops):
    n = w.shape[0]
    k, m = len(blocks), len(ins)

    def run(place_ref, w_ref, v_ref, *refs):
        bufs, sems = refs[-2:]
        copies = {}
        for i, r in enumerate(blocks):
            at = pl.ds(pl.multiple_of(place_ref[r] * n, n), n)
            for j, src in enumerate((w_ref, v_ref)):
                copies[i, j] = pltpu.make_async_copy(src.at[:, at], bufs.at[i, j], sems.at[i, j])
                copies[i, j].start()

        def get(i, j):
            copies[i, j].wait()
            return bufs[i, j]

        body(get, refs[:m], refs[m:-2])

    size = 2 * k * n * n * 2 + sum(a.size * a.dtype.itemsize for a in (*ins, *out))
    return pl.pallas_call(
        run,
        in_specs=[pl.BlockSpec(memory_space=pltpu.SMEM)]
        + [pl.BlockSpec(memory_space=pltpu.HBM)] * 2
        + [pl.BlockSpec(memory_space=pltpu.VMEM)] * m,
        out_specs=[pl.BlockSpec(memory_space=pltpu.VMEM)] * len(out),
        out_shape=out,
        scratch_shapes=[pltpu.VMEM((k, 2, n, n), BF), pltpu.SemaphoreType.DMA((k, 2))],
        compiler_params=pltpu.CompilerParams(vmem_limit_bytes=WEIGHT_LIMIT),
        cost_estimate=pl.CostEstimate(flops=flops, bytes_accessed=size, transcendentals=0),
    )(places, w, other, *ins)


def two(x_ref, x2_ref, get, i):
    return nn(x_ref[...], get(i, 0)) + nn(x2_ref[...], get(i, 1))


def first_body(get, ins, outs):
    outs[0][...] = two(*ins, get, 0).astype(BF)


def far_body(get, ins, outs):
    x, x2, from_z = ins
    to_left, to_right = outs
    n = from_z.shape[0]
    h = n // 2
    far = two(x, x2, get, 0) + from_z[...].astype(F32)
    to_left[n:] = far[h:].astype(BF)
    to_right[n:] = far[:h].astype(BF)
    to_left[:n] = two(x, x2, get, 1).astype(BF)
    to_right[:n] = two(x, x2, get, 2).astype(BF)


def near_body(get, ins, outs):
    x, x2, from_left, from_right = ins
    left, right, z = outs
    n = left.shape[0]
    h = n // 2
    a = two(x, x2, get, 0)
    left[:h] = a[:h].astype(BF)
    left[h:] = (a[h:] + from_right[n:].astype(F32)).astype(BF)
    b = two(x, x2, get, 1)
    right[:h] = (b[:h] + from_left[n:].astype(F32)).astype(BF)
    right[h:] = b[h:].astype(BF)
    c = two(x, x2, get, 2)
    z[...] = (c + from_left[:n].astype(F32) + from_right[:n].astype(F32)).astype(BF)


def last_body(a, b, c, own, out):
    total = own[...] + a[...].astype(F32) + b[...].astype(F32) + c[...].astype(F32)
    out[...] = total.astype(BF)


def back_near_body(get, ins, outs):
    total = [None, None]
    for i, part in enumerate(ins):
        for j in range(2):
            more = nt(part[...], get(i, j))
            total[j] = more if total[j] is None else total[j] + more
    for out, t in zip(outs, total):
        out[...] = t


def back_more_body(get, ins, outs):
    *parts, own, other = ins
    total = [own[...], other[...]]
    for i, part in enumerate(parts):
        rows = own.shape[0]
        for j in range(2):
            total[j] = total[j] + nt(part[:rows], get(i, j))
    for out, t in zip(outs, total):
        out[...] = t


def pack_body(z, left, right, to_left, to_right):
    n = z.shape[0]
    h = n // 2
    to_left[:n] = z[...]
    to_left[n:] = right[h:]
    to_right[:n] = z[...]
    to_right[n:] = left[:h]


def join_body(left, right, out):
    h = out.shape[0] // 2
    out[:h] = left[2 * h :]
    out[h:] = right[2 * h :]


def round_body(down, up, out):
    n = down.shape[0]
    out[:n] = down[...].astype(BF)
    out[n:] = up[...].astype(BF)


def group_body(own, left, right, far, out):
    n = own.shape[0] // 2
    for k in range(2):
        for i, a in enumerate((own, left, right, far)):
            out[(4 * k + i) * n : (4 * k + i + 1) * n] = a[k * n : (k + 1) * n]


def sum_body(a, b, out):
    out[...] = (a[...] + b[...].astype(F32)).astype(BF)


def adam_body(*refs):
    own, a, b, c = refs[:4]
    rows = own.shape[0] // 2
    ins, outs = refs[4:10], refs[10:]
    corr_one = 1.0 - 0.9**10
    corr_two = 1.0 - 0.999**10
    for k in range(2):
        at = slice(k * rows, (k + 1) * rows)
        grad = own[at] + a[at].astype(F32) + b[at].astype(F32) + c[at].astype(F32)
        param = ins[3 * k][...]
        first = 0.9 * ins[3 * k + 1][...] + 0.1 * grad
        second = 0.999 * ins[3 * k + 2][...] + 0.001 * grad * grad
        step = first / corr_one / (jnp.sqrt(second / corr_two) + 1e-08)
        outs[3 * k][...] = param - 0.01 * (step + 0.1 * param)
        outs[3 * k + 1][...] = first
        outs[3 * k + 2][...] = second


def tie(a, *before):
    return lax.optimization_barrier((a, *before))[0]


def local(x, w, dy, counts, slots, down, up, down_m, down_v, up_m, up_v):
    toks, n = x.shape
    per, rank = up.shape[0], up.shape[1]
    flat = per * rank
    n4 = 4 * flat
    half = toks // 2
    dot = 2 * toks * n * n
    block, wide = shape(toks, n, BF), shape(toks, n, F32)
    iy, iz, ix, il, ic = (lax.axis_index(a) for a in (*DP, *TENSOR))

    def down_rows(a):
        return jnp.transpose(a, (0, 2, 1)).reshape(flat, n)

    def up_rows(a):
        return a.reshape(flat, n)

    columns = [((ix + s) % 4) * 4 + ((il + t) % 2) * 2 + ic for t in (0, 1) for s in RING]
    places = jnp.stack(columns).astype(jnp.int32)

    pack = shape(toks + half, n, BF)

    def weighed(body, blocks, ins, out):
        return with_weight(body, blocks, w, other, places, ins, out, 2 * len(blocks) * dot)

    x2 = send(x, "c", 1)
    mine = call(round_body, [shape(2 * flat, n, BF)], (down_rows(down), up_rows(up)))[0]
    z_left, z_right, z_far = (send(tie(mine, x2), "zh", k) for k in (1, -1, 2))
    d_left, d_right = send(dy, "x", 1), send(dy, "x", -1)
    mask = token_mask(slots, counts, jnp.stack([iy, iz]).astype(jnp.int32), rank, per, toks)
    group = call(group_body, [shape(2 * n4, n, BF)], (tie(mine, mask), z_left, z_right, z_far))[0]
    y_left, y_right = send(group, "y", 1), send(group, "y", -1)
    other = send(tie(w, group, d_left, d_right), "c", 1)
    d_z = send(tie(dy, group), "zl", 1)
    zf = weighed(first_body, (7,), (x, x2), [block])[0]
    to_left, to_right = call(pack_body, [pack] * 2, (tie(d_z, y_left, y_right, zf), d_left, d_right))
    a_left, a_right = send(to_right, "x", 1), send(to_left, "x", -1)
    y_far_d = send(y_left[:n4], "y", 1)
    y_far_u = send(y_right[n4:], "y", -1)
    from_z = send(zf, "zl", 1)
    p_left, p_right = weighed(far_body, (3, 5, 6), (x, x2, tie(from_z, y_far_d, y_far_u)), [pack] * 2)
    adapters = (group, y_left, y_right, y_far_d, y_far_u)


    lb = call(
        functools.partial(narrow_body, rank),
        [shape(2 * rank, toks, F32)],
        (x, dy, tie(mask, p_left), *adapters),
        flops=4 * dot,
    )[0]
    lb = lb + send(lb, "c", 1)
    lb = tie(lb + send(lb, "zl", 1), a_left, a_right)
    near = weighed(back_near_body, (0, 1, 2, 4), (tie(dy, lb), d_left, d_right, d_z), [wide] * 2)
    lb = tie(lb, *near) + send(lb, "x", 1)
    d_far = call(join_body, [block], (tie(a_left, lb), a_right))[0]
    near = weighed(back_more_body, (3, 5, 6), (d_far, a_left, a_right, *near), [wide] * 2)
    lb = tie(lb, *near) + send(lb, "x", 2)

    fd, fu = call(
        functools.partial(grad_far_body, rank),
        [shape(n4, n, BF), shape(n4, n, BF)],
        (x, dy, mask, lb),
        flops=dot,
    )
    got_d, got_u = send(fd, "y", 1), send(fu, "y", -1)
    p_left, p_right, d_far_late = lax.optimization_barrier((p_left, p_right, d_far, lb))[:3]
    b_right, b_left = send(p_left, "x", -1), send(p_right, "x", 1)
    d_zf = send(d_far_late, "zl", 1)
    g_left, g_right = call(
        functools.partial(grad_near_body, rank),
        [shape(2 * n4, n, BF), shape(2 * n4, n, BF)],
        (x, dy, mask, lb, got_d, got_u),
        flops=2 * dot,
    )
    got_l, got_r = send(g_left, "y", -1), send(g_right, "y", 1)
    left, right, z = weighed(near_body, (1, 2, 4), (x, x2, tie(b_left, d_zf), b_right), [block] * 3)
    left, right = lax.optimization_barrier((left, right, got_l, got_r))[:2]
    sums = (send(left, "x", -1), send(right, "x", 1), send(z, "zl", 1))
    lifted, own_grad, to_other = weighed(
        functools.partial(back_body, rank),
        (0, 7),
        (
            x,
            x2,
            mask,
            lb,
            *adapters,
            tie(d_zf, left),
            *near,
        ),
        [wide, wide, block],
    )
    from_other = send(to_other, "c", 1)
    g_far, g_left, g_right, g_own = call(
        functools.partial(grad_own_body, rank),
        [shape(2 * flat, n, BF)] * 3 + [shape(2 * flat, n, F32)],
        (x, dy, mask, lb, tie(got_l, *sums, lifted), got_r),
        flops=dot,
    )
    from_far = send(g_far, "zh", 2)
    from_left, from_right = send(g_right, "zh", 1), send(g_left, "zh", -1)
    input_grad = call(sum_body, [block], (tie(own_grad, g_far), from_other))[0]

    new = call(
        adam_body,
        [shape(flat, n, F32)] * 6,
        (
            g_own,
            from_left,
            from_right,
            from_far,
            *(down_rows(a) for a in (down, down_m, down_v)),
            *(up_rows(a) for a in (up, up_m, up_v)),
        ),
    )
    new_down = [jnp.transpose(a.reshape(per, rank, n), (0, 2, 1)) for a in new[:3]]
    new_up = [a.reshape(per, rank, n) for a in new[3:]]
    proj_out = call(last_body, [block], (*sums, lifted))[0]
    return (
        proj_out,
        input_grad,
        new_down[0],
        new_up[0],
        new_down[1],
        new_down[2],
        new_up[1],
        new_up[2],
    )


def solution(mesh):
    torus = Mesh(mesh.devices.reshape(4, 4, 4, 2, 2), (*DP, *TENSOR))
    return jax.shard_map(
        local,
        mesh=torus,
        in_specs=(
            P(DP, TENSOR),
            P(TENSOR, None),
            P(DP, TENSOR),
            P(DP, None),
            P(),
            P(DP, TENSOR, None),
            P(DP, None, TENSOR),
            P(DP, TENSOR, None),
            P(DP, TENSOR, None),
            P(DP, None, TENSOR),
            P(DP, None, TENSOR),
        ),
        out_specs=(
            P(DP, TENSOR),
            P(DP, TENSOR),
            P(DP, TENSOR, None),
            P(DP, None, TENSOR),
            P(DP, TENSOR, None),
            P(DP, TENSOR, None),
            P(DP, None, TENSOR),
            P(DP, None, TENSOR),
        ),
        check_vma=False,
    )
```
